128 devices in a mesh: node: 8 (over x, core), local: 16 (over z, y).
Axes of the slice: x: 4, y: 4, z: 4, core: 2. Of those that a mesh axis runs over, the one named last changes fastest.
Arguments:
- tokens: bfloat16 [2048, 3584], P(('node', 'local')), may hold values from -6 to 6
- route: int32 [2048, 8], P(('node', 'local')), may hold values from 0 to 127, as said below
- combine_weight: bfloat16 [2048, 8], P(('node', 'local')), may hold values from 0.049804688 to 0.5
- gate_up: bfloat16 [128, 3584, 2048], P(('node', 'local')), may hold values from -0.09375 to 0.09375
- down: bfloat16 [128, 1024, 3584], P(('node', 'local')), may hold values from -0.1875 to 0.1875
Outputs:
- mixed: bfloat16 [2048, 3584], P(('node', 'local'))
The draws below stay inside these ranges and needn't reach their ends.
Inputs may be any that keep to these rules, and one draw needn't show every extreme that they name: `route`: expert e is held by device e in node-major order, so it lies on node e // 16. Each row names 8 different experts on exactly four nodes, two on each node. Among the rows of one device no expert is named more than 2 times; among the rows of the 8 devices that share one local index no expert is named more than 16 times; both bounds are reached in every draw.
All inputs are finite; a program needn't handle non-finite values.
Results may differ from the reference program's by a relative error of at most 0.012.
Values may be sent and summed in bfloat16 or wider, within the bound.
No kernel may reach another device: no remote copies, remote signals or barrier semaphores. Data moves between devices by JAX's collectives and lax.ppermute only.
A program may use at most 64 MiB of HBM per device.

```python
import math
import jax
import jax.numpy as jnp
from jax import lax

D = 3584
FF = 1024
TOPK = 8
TOK_DEV = 16
EXPERTS = 128
TOKENS = 2048
EXP_ROWS = 256
N_NODE = 8
N_LOCAL = 16


def draw_route(key, part):
    key = jax.random.fold_in(key, 7)
    node_keys = jax.random.split(jax.random.fold_in(key, 1), N_LOCAL)
    node_order = jax.vmap(lambda k: jax.random.permutation(k, N_NODE))(node_keys).astype(jnp.int32)
    local_keys = jax.random.split(jax.random.fold_in(key, 2), N_LOCAL * N_NODE)
    local_order = jax.vmap(lambda k: jax.random.permutation(k, N_LOCAL))(local_keys).astype(jnp.int32)
    local_order = local_order.reshape(N_LOCAL, N_NODE, N_LOCAL)
    template = jnp.concatenate([jnp.array([0, 1, 0], jnp.int32), jnp.arange(2, N_LOCAL - 1, dtype=jnp.int32)])
    row_index = jnp.arange(TOKENS, dtype=jnp.int32)
    device = row_index // TOK_DEV
    group_index = device % N_LOCAL
    member = device // N_LOCAL * TOK_DEV + row_index % TOK_DEV
    slot_index = member[:, None] * 4 + jnp.arange(4, dtype=jnp.int32)[None, :]
    residue = slot_index % N_NODE
    turn_index = slot_index // N_NODE
    node_pick = node_order[group_index[:, None], residue]
    position = 2 * turn_index[:, :, None] + jnp.arange(2, dtype=jnp.int32)[None, None, :]
    label_index = template[position % N_LOCAL]
    local_pick = local_order[group_index[:, None, None], node_pick[:, :, None], label_index]
    expert = node_pick[:, :, None] * N_LOCAL + local_pick
    return expert.reshape(TOKENS, 8).astype(jnp.int32)


def steps_of(stream_key, dims, pieces, smallest, top_value):
    loudness = 1.0
    for axis_at, parts in pieces:
        draws = jax.random.uniform(jax.random.fold_in(jax.random.fold_in(stream_key, 6), axis_at), (parts,), jnp.float32, smallest / len(pieces), top_value / len(pieces))
        loudness = loudness * jnp.repeat(jnp.exp(draws), dims[axis_at] // parts).reshape((-1,) + (1,) * (len(dims) - 1 - axis_at))
    return loudness


def scatter_about(own_key, dims, spread, reach, pieces=(), kind=jnp.bfloat16):
    values = spread * jax.random.normal(own_key, dims, jnp.float32)
    if pieces:
        values = values * steps_of(own_key, dims, pieces, -0.22, 0.18)
    return jnp.clip(values, -reach, reach).astype(kind)


def setup_inputs(seed: int = 0) -> dict:
    key_of = jax.random.split(jax.random.key(seed), 6)
    return {
        "tokens": scatter_about(key_of[0], (TOKENS, D), 1.0, 6.0, ((0, 128),)),
        "route": draw_route(jax.random.fold_in(key_of[5], 71), 0),
        "combine_weight": jnp.clip(jnp.exp(math.log(0.5) - 2.306499 * jax.random.uniform(key_of[2], (TOKENS, TOPK), jnp.float32) ** steps_of(key_of[2], (TOKENS, TOPK), ((0, 128),), -0.2, 0.2)), 0.049804688, 0.5).astype(jnp.bfloat16),
        "gate_up": scatter_about(key_of[3], (EXPERTS, D, 2 * FF), D ** -0.5, 0.09375, ((0, 128),)),
        "down": scatter_about(key_of[4], (EXPERTS, FF, D), FF ** -0.5, 0.1875, ((0, 128),)),
    }


def expert_rows(rows, gate_up, down):
    hidden_count = down.shape[0]
    hidden = jnp.dot(rows, gate_up, preferred_element_type=jnp.float32)
    active = (jax.nn.silu(hidden[:, :hidden_count]) * hidden[:, hidden_count:]).astype(jnp.bfloat16)
    return jnp.dot(active, down, preferred_element_type=jnp.float32).astype(jnp.bfloat16)


def node_combine(outputs, route, combine_weight, node_count, per_node):
    node_pick = route // per_node
    member = (node_pick[:, :, None] == jnp.arange(node_count, dtype=jnp.int32)[None, None, :]).astype(jnp.float32)
    coefficient = member * combine_weight.astype(jnp.float32)[:, :, None]
    partial_value = jnp.einsum("rkm,rkd->rmd", coefficient, outputs.astype(jnp.float32)).astype(jnp.bfloat16)
    return jnp.sum(partial_value.astype(jnp.float32), axis=1).astype(jnp.bfloat16)


def reference(tokens, route, combine_weight, gate_up, down):
    flat_route = route.reshape(-1)
    slot_count = flat_route.shape[0]
    top_count = route.shape[1]
    model_width = tokens.shape[1]

    def step_expert(carry, expert):
        hit_mask = flat_route == expert
        picked = jnp.nonzero(hit_mask, size=EXP_ROWS, fill_value=0)[0].astype(jnp.int32)
        is_live = jnp.arange(EXP_ROWS, dtype=jnp.int32) < jnp.sum(hit_mask.astype(jnp.int32))
        source = picked // top_count
        outputs = expert_rows(tokens[source], gate_up[expert], down[expert])
        target = jnp.where(is_live, picked, slot_count).astype(jnp.int32)
        return carry.at[target].set(outputs, mode="drop"), None

    empty_rows = jnp.zeros((slot_count, model_width), jnp.bfloat16)
    outputs, _ = lax.scan(step_expert, empty_rows, jnp.arange(gate_up.shape[0], dtype=jnp.int32))
    return node_combine(outputs.reshape(-1, top_count, model_width), route, combine_weight, N_NODE, N_LOCAL)
```

```python
import functools

import jax
import jax.numpy as jnp
from jax import lax
from jax.experimental import pallas as pl
from jax.experimental.pallas import tpu as pltpu
from jax.sharding import PartitionSpec as P

LANES = 128
F32 = jnp.float32
BF16 = jnp.bfloat16


def pack_kernel(route_ref, tokens_ref, out_ref, rank_ref, low, high, source):
    top_count, row_count = route_ref.shape
    chunks = tokens_ref.shape[1] // LANES
    pitch = 2 * chunks
    peers = out_ref.shape[0] // pitch

    low[...] = jnp.zeros_like(low)
    high[...] = jnp.zeros_like(high)
    for c in range(chunks):
        part = tokens_ref[:, c * LANES : (c + 1) * LANES].astype(F32)
        low[pl.ds(2 * c, row_count, stride=pitch), :] = part
        high[pl.ds(2 * c + 1, row_count, stride=pitch), :] = part

    def clear(i, _):
        source[i] = row_count
        return 0

    lax.fori_loop(0, 2 * peers, clear, 0, unroll=16)

    def place(t, _):
        for k in range(top_count):
            e = route_ref[k, t]
            r = jnp.where(source[e] == row_count, 0, 1)
            source[r * peers + e] = t
            rank_ref[k, t] = r
        return 0

    lax.fori_loop(0, row_count, place, 0)

    def fill(i, _):
        blocks = []
        for p in (2 * i, 2 * i + 1):
            a = pl.multiple_of(source[p] * pitch, 8)
            b = pl.multiple_of(source[peers + p] * pitch, 8)
            blocks.append(low[pl.ds(a, pitch), :] + high[pl.ds(b, pitch), :])
        out_ref[pl.ds(pl.multiple_of(i * 2 * pitch, 16), 2 * pitch), :] = jnp.concatenate(
            blocks, axis=0
        ).astype(BF16)
        return 0

    lax.fori_loop(0, peers // 2, fill, 0, unroll=2)


def pack(route, tokens, peers):
    row_count, width = tokens.shape
    pitch = 2 * width // LANES
    return pl.pallas_call(
        pack_kernel,
        out_shape=(
            jax.ShapeDtypeStruct((peers * pitch, LANES), BF16),
            jax.ShapeDtypeStruct(route.shape, jnp.int32),
        ),
        in_specs=[
            pl.BlockSpec(memory_space=pltpu.SMEM),
            pl.BlockSpec(memory_space=pltpu.VMEM),
        ],
        out_specs=(
            pl.BlockSpec(memory_space=pltpu.VMEM),
            pl.BlockSpec(memory_space=pltpu.SMEM),
        ),
        scratch_shapes=[
            pltpu.VMEM(((row_count + 1) * pitch, LANES), F32),
            pltpu.VMEM(((row_count + 1) * pitch, LANES), F32),
            pltpu.SMEM((2 * peers,), jnp.int32),
        ],
        compiler_params=pltpu.CompilerParams(vmem_limit_bytes=16 * 2**20),
        name="pack",
    )(route, tokens)


UP_TILE = 256
DOWN_TILE = 512


def ffn_kernel(
    got_ref, gate_up_ref, down_ref, out_ref, raw, wide, rows, gate_up, down, active, got_sem, up_sem, down_sem
):
    width = rows.shape[1]
    hidden = active.shape[1]
    chunks = width // LANES
    pitch = 2 * chunks
    peers = raw.shape[0] // pitch
    up_steps = hidden // UP_TILE
    down_steps = width // DOWN_TILE

    def up_copy(n):
        half, step = n % 2, n // 2
        return pltpu.make_async_copy(
            gate_up_ref.at[0, :, pl.ds(half * hidden + step * UP_TILE, UP_TILE)],
            gate_up.at[n],
            up_sem.at[n],
        )

    def down_copy(n):
        return pltpu.make_async_copy(
            down_ref.at[0, :, pl.ds(n * DOWN_TILE, DOWN_TILE)], down.at[n], down_sem.at[n]
        )

    got = pltpu.make_async_copy(got_ref, raw, got_sem)
    got.start()
    for n in range(2 * up_steps):
        up_copy(n).start()
    for n in range(down_steps):
        down_copy(n).start()
    got.wait()

    piece = 512

    def widen(i, _):
        span = pl.ds(pl.multiple_of(i * piece, piece), piece)
        wide[span, :] = raw[span, :].astype(F32)
        return 0

    lax.fori_loop(0, peers * pitch // piece, widen, 0)
    for c in range(chunks):
        for r in range(2):
            rows[r * peers : (r + 1) * peers, c * LANES : (c + 1) * LANES] = wide[
                pl.ds(2 * c + r, peers, stride=pitch), :
            ].astype(BF16)

    for step in range(up_steps):
        up_copy(2 * step).wait()
        gate = jnp.dot(rows[...], gate_up[2 * step], preferred_element_type=F32)
        up_copy(2 * step + 1).wait()
        up = jnp.dot(rows[...], gate_up[2 * step + 1], preferred_element_type=F32)
        active[:, step * UP_TILE : (step + 1) * UP_TILE] = (gate / (1 + jnp.exp(-gate)) * up).astype(BF16)

    for step in range(down_steps):
        down_copy(step).wait()
        result = jnp.dot(active[...], down[step], preferred_element_type=F32)
        for q in range(DOWN_TILE // LANES):
            c = step * (DOWN_TILE // LANES) + q
            for r in range(2):
                wide[pl.ds(2 * c + r, peers, stride=pitch), :] = result[
                    r * peers : (r + 1) * peers, q * LANES : (q + 1) * LANES
                ]

    def narrow(i, _):
        span = pl.ds(pl.multiple_of(i * piece, piece), piece)
        out_ref[span, :] = wide[span, :].astype(BF16)
        return 0

    lax.fori_loop(0, peers * pitch // piece, narrow, 0)


def expert_ffn(got, gate_up, down):
    _, width, both = gate_up.shape
    hidden = both // 2
    total = got.shape[0]
    slots = total * LANES // width
    up_steps = 2 * hidden // UP_TILE
    down_steps = width // DOWN_TILE
    return pl.pallas_call(
        ffn_kernel,
        out_shape=jax.ShapeDtypeStruct(got.shape, BF16),
        in_specs=[pl.BlockSpec(memory_space=pl.ANY)] * 3,
        out_specs=pl.BlockSpec(memory_space=pltpu.VMEM),
        scratch_shapes=[
            pltpu.VMEM((total, LANES), BF16),
            pltpu.VMEM((total, LANES), F32),
            pltpu.VMEM((slots, width), BF16),
            pltpu.VMEM((up_steps, width, UP_TILE), BF16),
            pltpu.VMEM((down_steps, hidden, DOWN_TILE), BF16),
            pltpu.VMEM((slots, hidden), BF16),
            pltpu.SemaphoreType.DMA,
            pltpu.SemaphoreType.DMA((up_steps,)),
            pltpu.SemaphoreType.DMA((down_steps,)),
        ],
        compiler_params=pltpu.CompilerParams(vmem_limit_bytes=44 * 2**20),
        cost_estimate=pl.CostEstimate(
            flops=2 * slots * width * hidden * 3, bytes_accessed=6 * width * hidden, transcendentals=slots * hidden
        ),
        name="expert_ffn",
    )(got, gate_up, down)


def combine_kernel(route_ref, rank_ref, weight_ref, got_ref, out_ref, wide, total):
    top_count, row_count = route_ref.shape
    chunks = out_ref.shape[1] // LANES
    pitch = 2 * chunks
    peers = got_ref.shape[0] // pitch
    piece = 512

    def widen(i, _):
        span = pl.ds(pl.multiple_of(i * piece, piece), piece)
        wide[span, :] = got_ref[span, :].astype(F32)
        return 0

    lax.fori_loop(0, peers * pitch // piece, widen, 0)
    parity = lax.broadcasted_iota(jnp.int32, (8, LANES), 0) % 2

    def add_up(t, _):
        acc = jnp.zeros((pitch // 8, 8, LANES), F32)
        for k in range(top_count):
            start = pl.multiple_of(route_ref[k, t] * pitch, 8)
            scale = jnp.where(parity == rank_ref[k, t], weight_ref[k, t], 0.0)
            acc += wide[pl.ds(start, pitch), :].reshape(pitch // 8, 8, LANES) * scale[None]
        total[pl.ds(pl.multiple_of(t * pitch, 8), pitch), :] = acc.reshape(pitch, LANES)
        return 0

    lax.fori_loop(0, row_count, add_up, 0)
    for c in range(chunks):
        out_ref[:, c * LANES : (c + 1) * LANES] = (
            total[pl.ds(2 * c, row_count, stride=pitch), :] + total[pl.ds(2 * c + 1, row_count, stride=pitch), :]
        ).astype(BF16)


def combine(route, rank, weight, got, width):
    row_count = route.shape[1]
    pitch = 2 * width // LANES
    smem = pl.BlockSpec(memory_space=pltpu.SMEM)
    vmem = pl.BlockSpec(memory_space=pltpu.VMEM)
    return pl.pallas_call(
        combine_kernel,
        out_shape=jax.ShapeDtypeStruct((row_count, width), BF16),
        in_specs=[smem, smem, smem, vmem],
        out_specs=vmem,
        scratch_shapes=[
            pltpu.VMEM(got.shape, F32),
            pltpu.VMEM((row_count * pitch, LANES), F32),
        ],
        compiler_params=pltpu.CompilerParams(vmem_limit_bytes=24 * 2**20),
        name="combine",
    )(route, rank, weight, got)


def exchange(blocks, peers):
    shape = blocks.shape
    blocks = blocks.reshape(peers, -1, LANES)
    return lax.all_to_all(blocks, ("node", "local"), split_axis=0, concat_axis=0, tiled=True).reshape(shape)


def on_device(tokens, route, combine_weight, gate_up, down):
    width = tokens.shape[1]
    peers = lax.axis_size("node") * lax.axis_size("local")
    route = route.T
    weight = combine_weight.T.astype(F32)
    send, rank = pack(route, tokens, peers)
    got = exchange(send, peers)
    result = expert_ffn(got, gate_up, down)
    back = exchange(result, peers)
    return combine(route, rank, weight, back, width)


def solution(mesh):
    spec = P(("node", "local"), None)
    weights = P(("node", "local"), None, None)
    return jax.shard_map(
        on_device,
        mesh=mesh,
        in_specs=(spec, spec, spec, weights, weights),
        out_specs=spec,
        check_vma=False,
    )
```

```python
import jax
import jax.numpy as jnp
from jax import lax
from jax.experimental import pallas as pl
from jax.experimental.pallas import tpu as pltpu
from jax.sharding import PartitionSpec as P

LANES = 128
F32 = jnp.float32
BF16 = jnp.bfloat16


def pack_kernel(route_ref, tokens_ref, out_ref, rank_ref, low, high, source):
    top_count, row_count = route_ref.shape
    chunks = tokens_ref.shape[1] // LANES
    pitch = 2 * chunks
    peers = out_ref.shape[0] // pitch

    low[...] = jnp.zeros_like(low)
    high[...] = jnp.zeros_like(high)
    for c in range(chunks):
        part = tokens_ref[:, c * LANES : (c + 1) * LANES].astype(F32)
        low[pl.ds(2 * c, row_count, stride=pitch), :] = part
        high[pl.ds(2 * c + 1, row_count, stride=pitch), :] = part

    def clear(i, _):
        source[i] = row_count
        return 0

    lax.fori_loop(0, 2 * peers, clear, 0, unroll=16)

    def place(t, _):
        for k in range(top_count):
            e = route_ref[k, t]
            r = jnp.where(source[e] == row_count, 0, 1)
            source[r * peers + e] = t
            rank_ref[k, t] = r
        return 0

    lax.fori_loop(0, row_count, place, 0)

    def fill(i, _):
        blocks = []
        for p in (2 * i, 2 * i + 1):
            a = pl.multiple_of(source[p] * pitch, 8)
            b = pl.multiple_of(source[peers + p] * pitch, 8)
            blocks.append(low[pl.ds(a, pitch), :] + high[pl.ds(b, pitch), :])
        out_ref[pl.ds(pl.multiple_of(i * 2 * pitch, 16), 2 * pitch), :] = jnp.concatenate(
            blocks, axis=0
        ).astype(BF16)
        return 0

    lax.fori_loop(0, peers // 2, fill, 0, unroll=2)


def pack(route, tokens, peers):
    row_count, width = tokens.shape
    pitch = 2 * width // LANES
    return pl.pallas_call(
        pack_kernel,
        out_shape=(
            jax.ShapeDtypeStruct((peers * pitch, LANES), BF16),
            jax.ShapeDtypeStruct(route.shape, jnp.int32),
        ),
        in_specs=[
            pl.BlockSpec(memory_space=pltpu.SMEM),
            pl.BlockSpec(memory_space=pltpu.VMEM),
        ],
        out_specs=(
            pl.BlockSpec(memory_space=pltpu.VMEM),
            pl.BlockSpec(memory_space=pltpu.SMEM),
        ),
        scratch_shapes=[
            pltpu.VMEM(((row_count + 1) * pitch, LANES), F32),
            pltpu.VMEM(((row_count + 1) * pitch, LANES), F32),
            pltpu.SMEM((2 * peers,), jnp.int32),
        ],
        compiler_params=pltpu.CompilerParams(vmem_limit_bytes=16 * 2**20),
        name="pack",
    )(route, tokens)


UP_TILE = 256
DOWN_TILE = 512
DOWN_GROUP = 4
IN_FLIGHT = 6
PIECE = 512


def ffn_kernel(got_ref, gate_up_ref, down_ref, out_ref, wide, rows, gate_up, down, active, up_sem, down_sem):
    width = rows.shape[1]
    hidden = active.shape[1]
    chunks = width // LANES
    pitch = 2 * chunks
    peers = got_ref.shape[0] // pitch
    up_steps = hidden // UP_TILE
    down_steps = width // DOWN_TILE

    copies = []
    for n in range(2 * up_steps):
        start = n % 2 * hidden + n // 2 * UP_TILE
        copies.append(
            pltpu.make_async_copy(
                gate_up_ref.at[0, :, pl.ds(start, UP_TILE)], gate_up.at[n], up_sem.at[n]
            )
        )
    for n in range(down_steps):
        copies.append(
            pltpu.make_async_copy(
                down_ref.at[0, :, pl.ds(n * DOWN_TILE, DOWN_TILE)], down.at[n], down_sem.at[n]
            )
        )
    for copy in copies[:IN_FLIGHT]:
        copy.start()

    def take(n):
        copies[n].wait()
        if n + IN_FLIGHT < len(copies):
            copies[n + IN_FLIGHT].start()

    def widen(i, _):
        span = pl.ds(pl.multiple_of(i * PIECE, PIECE), PIECE)
        wide[span, :] = got_ref[span, :].astype(F32)
        return 0

    lax.fori_loop(0, peers * pitch // PIECE, widen, 0)
    for c in range(chunks):
        for r in range(2):
            rows[r * peers : (r + 1) * peers, c * LANES : (c + 1) * LANES] = wide[
                pl.ds(2 * c + r, peers, stride=pitch), :
            ].astype(BF16)

    for step in range(up_steps):
        take(2 * step)
        take(2 * step + 1)
        gate = jnp.dot(rows[...], gate_up[2 * step], preferred_element_type=F32)
        up = jnp.dot(rows[...], gate_up[2 * step + 1], preferred_element_type=F32)
        active[:, step * UP_TILE : (step + 1) * UP_TILE] = (gate / (1 + jnp.exp(-gate)) * up).astype(BF16)

    for first in range(0, down_steps, DOWN_GROUP):
        steps = range(first, min(first + DOWN_GROUP, down_steps))
        for step in steps:
            take(2 * up_steps + step)
        for step in steps:
            result = jnp.dot(active[...], down[step], preferred_element_type=F32)
            for q in range(DOWN_TILE // LANES):
                c = step * (DOWN_TILE // LANES) + q
                for r in range(2):
                    wide[pl.ds(2 * c + r, peers, stride=pitch), :] = result[
                        r * peers : (r + 1) * peers, q * LANES : (q + 1) * LANES
                    ]

    def narrow(i, _):
        span = pl.ds(pl.multiple_of(i * PIECE, PIECE), PIECE)
        out_ref[span, :] = wide[span, :].astype(BF16)
        return 0

    lax.fori_loop(0, peers * pitch // PIECE, narrow, 0)


def expert_ffn(got, gate_up, down):
    _, width, both = gate_up.shape
    hidden = both // 2
    total = got.shape[0]
    slots = total * LANES // width
    up_tiles = both // UP_TILE
    down_tiles = width // DOWN_TILE
    return pl.pallas_call(
        ffn_kernel,
        out_shape=jax.ShapeDtypeStruct(got.shape, BF16),
        in_specs=[
            pl.BlockSpec(memory_space=pltpu.VMEM),
            pl.BlockSpec(memory_space=pl.ANY),
            pl.BlockSpec(memory_space=pl.ANY),
        ],
        out_specs=pl.BlockSpec(memory_space=pltpu.VMEM),
        scratch_shapes=[
            pltpu.VMEM((total, LANES), F32),
            pltpu.VMEM((slots, width), BF16),
            pltpu.VMEM((up_tiles, width, UP_TILE), BF16),
            pltpu.VMEM((down_tiles, hidden, DOWN_TILE), BF16),
            pltpu.VMEM((slots, hidden), BF16),
            pltpu.SemaphoreType.DMA((up_tiles,)),
            pltpu.SemaphoreType.DMA((down_tiles,)),
        ],
        compiler_params=pltpu.CompilerParams(vmem_limit_bytes=44 * 2**20),
        cost_estimate=pl.CostEstimate(
            flops=2 * slots * width * hidden * 3, bytes_accessed=6 * width * hidden, transcendentals=slots * hidden
        ),
        name="expert_ffn",
    )(got, gate_up, down)


def combine_kernel(route_ref, rank_ref, weight_ref, got_ref, out_ref, wide, total):
    top_count, row_count = route_ref.shape
    chunks = out_ref.shape[1] // LANES
    pitch = 2 * chunks
    peers = got_ref.shape[0] // pitch
    def widen(i, _):
        span = pl.ds(pl.multiple_of(i * PIECE, PIECE), PIECE)
        wide[span, :] = got_ref[span, :].astype(F32)
        return 0

    lax.fori_loop(0, peers * pitch // PIECE, widen, 0)
    parity = lax.broadcasted_iota(jnp.int32, (8, LANES), 0) % 2

    def add_up(t, _):
        acc = jnp.zeros((pitch // 8, 8, LANES), F32)
        for k in range(top_count):
            start = pl.multiple_of(route_ref[k, t] * pitch, 8)
            scale = jnp.where(parity == rank_ref[k, t], weight_ref[k, t], 0.0)
            acc += wide[pl.ds(start, pitch), :].reshape(pitch // 8, 8, LANES) * scale[None]
        total[pl.ds(pl.multiple_of(t * pitch, 8), pitch), :] = acc.reshape(pitch, LANES)
        return 0

    lax.fori_loop(0, row_count, add_up, 0)
    for c in range(chunks):
        out_ref[:, c * LANES : (c + 1) * LANES] = (
            total[pl.ds(2 * c, row_count, stride=pitch), :] + total[pl.ds(2 * c + 1, row_count, stride=pitch), :]
        ).astype(BF16)


def combine(route, rank, weight, got, width):
    row_count = route.shape[1]
    pitch = 2 * width // LANES
    smem = pl.BlockSpec(memory_space=pltpu.SMEM)
    vmem = pl.BlockSpec(memory_space=pltpu.VMEM)
    return pl.pallas_call(
        combine_kernel,
        out_shape=jax.ShapeDtypeStruct((row_count, width), BF16),
        in_specs=[smem, smem, smem, vmem],
        out_specs=vmem,
        scratch_shapes=[
            pltpu.VMEM(got.shape, F32),
            pltpu.VMEM((row_count * pitch, LANES), F32),
        ],
        compiler_params=pltpu.CompilerParams(vmem_limit_bytes=24 * 2**20),
        name="combine",
    )(route, rank, weight, got)


def exchange(blocks, peers):
    shape = blocks.shape
    blocks = blocks.reshape(peers, -1, LANES)
    return lax.all_to_all(blocks, ("node", "local"), split_axis=0, concat_axis=0, tiled=True).reshape(shape)


def on_device(tokens, route, combine_weight, gate_up, down):
    width = tokens.shape[1]
    peers = lax.axis_size("node") * lax.axis_size("local")
    route = route.T
    weight = combine_weight.T.astype(F32)
    send, rank = pack(route, tokens, peers)
    got = exchange(send, peers)
    result = expert_ffn(got, gate_up, down)
    back = exchange(result, peers)
    return combine(route, rank, weight, back, width)


def solution(mesh):
    spec = P(("node", "local"), None)
    weights = P(("node", "local"), None, None)
    return jax.shard_map(
        on_device,
        mesh=mesh,
        in_specs=(spec, spec, spec, weights, weights),
        out_specs=spec,
        check_vma=False,
    )
```

```python
import jax
import jax.numpy as jnp
from jax import lax
from jax.experimental import pallas as pl
from jax.experimental.pallas import tpu as pltpu
from jax.sharding import PartitionSpec as P

LANES = 128
F32 = jnp.float32
BF16 = jnp.bfloat16


PACK_STEPS = 8


def pack_kernel(
    route_ref, tokens_ref, out_ref, first_ref, route, tokens, blocks, first, low, high, source, in_sem, out_sem
):
    top_count, row_count = route.shape
    chunks = tokens.shape[1] // LANES
    pitch = 2 * chunks
    peers = blocks.shape[0] // pitch
    step_peers = peers // PACK_STEPS

    fetch_route = pltpu.make_async_copy(route_ref, route, in_sem.at[0])
    fetch_tokens = pltpu.make_async_copy(tokens_ref, tokens, in_sem.at[1])
    fetch_route.start()
    fetch_tokens.start()
    low[...] = jnp.zeros_like(low)
    high[...] = jnp.zeros_like(high)
    fetch_route.wait()

    peer = lax.broadcasted_iota(jnp.int32, (top_count, peers), 1)
    lowest = jnp.full((top_count, peers), row_count, jnp.int32)
    highest = jnp.full((top_count, peers), -1, jnp.int32)
    for t in range(row_count):
        named = route[:, t : t + 1] == peer
        lowest = jnp.where(named, jnp.minimum(lowest, t), lowest)
        highest = jnp.where(named, t, highest)
    lowest = jnp.min(lowest, axis=0, keepdims=True)
    highest = jnp.max(highest, axis=0, keepdims=True)
    second = jnp.where(highest > lowest, highest, row_count)
    side = lax.broadcasted_iota(jnp.int32, (8, peers), 0)
    first[...] = jnp.where(side == 0, lowest, second)
    publish = pltpu.make_async_copy(first, source, in_sem.at[2])
    publish.start()
    keep = pltpu.make_async_copy(first, first_ref, in_sem.at[3])
    keep.start()
    fetch_tokens.wait()
    for c in range(chunks):
        part = tokens[:, c * LANES : (c + 1) * LANES].astype(F32)
        low[pl.ds(2 * c, row_count, stride=pitch), :] = part
        high[pl.ds(2 * c + 1, row_count, stride=pitch), :] = part
    publish.wait()

    def fill(i, _):
        pair = []
        for p in (2 * i, 2 * i + 1):
            a = pl.multiple_of(source[0, p] * pitch, 8)
            b = pl.multiple_of(source[1, p] * pitch, 8)
            pair.append(low[pl.ds(a, pitch), :] + high[pl.ds(b, pitch), :])
        blocks[pl.ds(pl.multiple_of(i * 2 * pitch, 16), 2 * pitch), :] = jnp.concatenate(
            pair, axis=0
        ).astype(BF16)
        return 0

    sends = []
    for step in range(PACK_STEPS):
        lax.fori_loop(step * step_peers // 2, (step + 1) * step_peers // 2, fill, 0, unroll=4)
        span = pl.ds(step * step_peers * pitch, step_peers * pitch)
        sends.append(pltpu.make_async_copy(blocks.at[span], out_ref.at[span], out_sem.at[step]))
        sends[step].start()
    keep.wait()
    for send in sends:
        send.wait()


def pack(route, tokens, peers):
    row_count, width = tokens.shape
    pitch = 2 * width // LANES
    anywhere = pl.BlockSpec(memory_space=pl.ANY)
    return pl.pallas_call(
        pack_kernel,
        out_shape=(
            jax.ShapeDtypeStruct((peers * pitch, LANES), BF16),
            jax.ShapeDtypeStruct((8, peers), jnp.int32),
        ),
        in_specs=[anywhere, anywhere],
        out_specs=(anywhere, anywhere),
        scratch_shapes=[
            pltpu.VMEM(route.shape, jnp.int32),
            pltpu.VMEM(tokens.shape, BF16),
            pltpu.VMEM((peers * pitch, LANES), BF16),
            pltpu.VMEM((8, peers), jnp.int32),
            pltpu.VMEM(((row_count + 1) * pitch, LANES), F32),
            pltpu.VMEM(((row_count + 1) * pitch, LANES), F32),
            pltpu.SMEM((8, peers), jnp.int32),
            pltpu.SemaphoreType.DMA((4,)),
            pltpu.SemaphoreType.DMA((PACK_STEPS,)),
        ],
        compiler_params=pltpu.CompilerParams(vmem_limit_bytes=60000000),
        name="pack",
    )(route, tokens)


UP_TILE = 256
DOWN_TILE = 512
DOWN_GROUP = 4
IN_FLIGHT = 6
PIECE = 512


def ffn_kernel(got_ref, gate_up_ref, down_ref, out_ref, wide, rows, gate_up, down, active, up_sem, down_sem):
    width = rows.shape[1]
    hidden = active.shape[1]
    chunks = width // LANES
    pitch = 2 * chunks
    peers = got_ref.shape[0] // pitch
    up_steps = hidden // UP_TILE
    down_steps = width // DOWN_TILE

    copies = []
    for n in range(2 * up_steps):
        start = n % 2 * hidden + n // 2 * UP_TILE
        copies.append(
            pltpu.make_async_copy(
                gate_up_ref.at[0, :, pl.ds(start, UP_TILE)], gate_up.at[n], up_sem.at[n]
            )
        )
    for n in range(down_steps):
        copies.append(
            pltpu.make_async_copy(
                down_ref.at[0, :, pl.ds(n * DOWN_TILE, DOWN_TILE)], down.at[n], down_sem.at[n]
            )
        )
    for copy in copies[:IN_FLIGHT]:
        copy.start()

    def take(n):
        copies[n].wait()
        if n + IN_FLIGHT < len(copies):
            copies[n + IN_FLIGHT].start()

    def widen(i, _):
        span = pl.ds(pl.multiple_of(i * PIECE, PIECE), PIECE)
        wide[span, :] = got_ref[span, :].astype(F32)
        return 0

    lax.fori_loop(0, peers * pitch // PIECE, widen, 0)
    for c in range(chunks):
        for r in range(2):
            rows[r * peers : (r + 1) * peers, c * LANES : (c + 1) * LANES] = wide[
                pl.ds(2 * c + r, peers, stride=pitch), :
            ].astype(BF16)

    for step in range(up_steps):
        take(2 * step)
        take(2 * step + 1)
        gate = jnp.dot(rows[...], gate_up[2 * step], preferred_element_type=F32)
        up = jnp.dot(rows[...], gate_up[2 * step + 1], preferred_element_type=F32)
        active[:, step * UP_TILE : (step + 1) * UP_TILE] = (gate / (1 + jnp.exp(-gate)) * up).astype(BF16)

    for first in range(0, down_steps, DOWN_GROUP):
        steps = range(first, min(first + DOWN_GROUP, down_steps))
        for step in steps:
            take(2 * up_steps + step)
        for step in steps:
            result = jnp.dot(active[...], down[step], preferred_element_type=F32)
            for q in range(DOWN_TILE // LANES):
                c = step * (DOWN_TILE // LANES) + q
                for r in range(2):
                    wide[pl.ds(2 * c + r, peers, stride=pitch), :] = result[
                        r * peers : (r + 1) * peers, q * LANES : (q + 1) * LANES
                    ]

    def narrow(i, _):
        span = pl.ds(pl.multiple_of(i * PIECE, PIECE), PIECE)
        out_ref[span, :] = wide[span, :].astype(BF16)
        return 0

    lax.fori_loop(0, peers * pitch // PIECE, narrow, 0)


def expert_ffn(got, gate_up, down):
    _, width, both = gate_up.shape
    hidden = both // 2
    total = got.shape[0]
    slots = total * LANES // width
    up_tiles = both // UP_TILE
    down_tiles = width // DOWN_TILE
    return pl.pallas_call(
        ffn_kernel,
        out_shape=jax.ShapeDtypeStruct(got.shape, BF16),
        in_specs=[
            pl.BlockSpec(memory_space=pltpu.VMEM),
            pl.BlockSpec(memory_space=pl.ANY),
            pl.BlockSpec(memory_space=pl.ANY),
        ],
        out_specs=pl.BlockSpec(memory_space=pltpu.VMEM),
        scratch_shapes=[
            pltpu.VMEM((total, LANES), F32),
            pltpu.VMEM((slots, width), BF16),
            pltpu.VMEM((up_tiles, width, UP_TILE), BF16),
            pltpu.VMEM((down_tiles, hidden, DOWN_TILE), BF16),
            pltpu.VMEM((slots, hidden), BF16),
            pltpu.SemaphoreType.DMA((up_tiles,)),
            pltpu.SemaphoreType.DMA((down_tiles,)),
        ],
        compiler_params=pltpu.CompilerParams(vmem_limit_bytes=44 * 2**20),
        cost_estimate=pl.CostEstimate(
            flops=2 * slots * width * hidden * 3, bytes_accessed=6 * width * hidden, transcendentals=slots * hidden
        ),
        name="expert_ffn",
    )(got, gate_up, down)


def combine_kernel(
    route_ref, first_ref, weight_ref, got_ref, out_ref, wide, total, narrow, scale, route, first, weight, sem
):
    top_count, row_count = route.shape
    chunks = out_ref.shape[1] // LANES
    pitch = 2 * chunks
    peers = got_ref.shape[0] // pitch

    fetch_weight = pltpu.make_async_copy(weight_ref, narrow, sem.at[0])
    fetch_route = pltpu.make_async_copy(route_ref, route, sem.at[1])
    fetch_first = pltpu.make_async_copy(first_ref, first, sem.at[2])
    fetch_weight.start()
    fetch_route.start()
    fetch_first.start()

    def widen(i, _):
        span = pl.ds(pl.multiple_of(i * PIECE, PIECE), PIECE)
        wide[span, :] = got_ref[span, :].astype(F32)
        return 0

    pieces = peers * pitch // PIECE
    lax.fori_loop(0, pieces // 2, widen, 0)
    fetch_weight.wait()
    scale[...] = narrow[...].astype(F32)
    publish = pltpu.make_async_copy(scale, weight, sem.at[3])
    publish.start()
    lax.fori_loop(pieces // 2, pieces, widen, 0)
    fetch_route.wait()
    fetch_first.wait()
    publish.wait()
    parity = lax.broadcasted_iota(jnp.int32, (8, LANES), 0) % 2

    def add_up(t, _):
        acc = jnp.zeros((pitch // 8, 8, LANES), F32)
        for k in range(top_count):
            e = route[k, t]
            start = pl.multiple_of(e * pitch, 8)
            rank = jnp.where(first[0, e] == t, 0, 1)
            factor = jnp.where(parity == rank, weight[k, t], 0.0)
            acc += wide[pl.ds(start, pitch), :].reshape(pitch // 8, 8, LANES) * factor[None]
        total[pl.ds(pl.multiple_of(t * pitch, 8), pitch), :] = acc.reshape(pitch, LANES)
        return 0

    lax.fori_loop(0, row_count, add_up, 0, unroll=4)
    for c in range(chunks):
        out_ref[:, c * LANES : (c + 1) * LANES] = (
            total[pl.ds(2 * c, row_count, stride=pitch), :] + total[pl.ds(2 * c + 1, row_count, stride=pitch), :]
        ).astype(BF16)


def combine(route, first, weight, got, width):
    row_count = route.shape[1]
    pitch = 2 * width // LANES
    anywhere = pl.BlockSpec(memory_space=pl.ANY)
    vmem = pl.BlockSpec(memory_space=pltpu.VMEM)
    return pl.pallas_call(
        combine_kernel,
        out_shape=jax.ShapeDtypeStruct((row_count, width), BF16),
        in_specs=[anywhere, anywhere, anywhere, vmem],
        out_specs=vmem,
        scratch_shapes=[
            pltpu.VMEM(got.shape, F32),
            pltpu.VMEM((row_count * pitch, LANES), F32),
            pltpu.VMEM(weight.shape, BF16),
            pltpu.VMEM(weight.shape, F32),
            pltpu.SMEM(route.shape, jnp.int32),
            pltpu.SMEM(first.shape, jnp.int32),
            pltpu.SMEM(weight.shape, F32),
            pltpu.SemaphoreType.DMA((4,)),
        ],
        compiler_params=pltpu.CompilerParams(vmem_limit_bytes=24 * 2**20),
        name="combine",
    )(route, first, weight, got)


def exchange(blocks, peers):
    shape = blocks.shape
    blocks = blocks.reshape(peers, -1, LANES)
    return lax.all_to_all(blocks, ("node", "local"), split_axis=0, concat_axis=0, tiled=True).reshape(shape)


def on_device(tokens, route, combine_weight, gate_up, down):
    width = tokens.shape[1]
    peers = lax.axis_size("node") * lax.axis_size("local")
    route = route.T
    send, first = pack(route, tokens, peers)
    got = exchange(send, peers)
    result = expert_ffn(got, gate_up, down)
    back = exchange(result, peers)
    return combine(route, first, combine_weight.T, back, width)


def solution(mesh):
    spec = P(("node", "local"), None)
    weights = P(("node", "local"), None, None)
    return jax.shard_map(
        on_device,
        mesh=mesh,
        in_specs=(spec, spec, spec, weights, weights),
        out_specs=spec,
        check_vma=False,
    )
```

```python
import jax
import jax.numpy as jnp
from jax import lax
from jax.experimental import pallas as pl
from jax.experimental.pallas import tpu as pltpu
from jax.sharding import PartitionSpec as P

LANES = 128
F32 = jnp.float32
BF16 = jnp.bfloat16
UP_TILE = 256
HEAD = 2
DOWN_TILE = 512
DOWN_GROUP = 4
IN_FLIGHT = 6
PIECE = 512


def up_start(n, hidden):
    return n % 2 * hidden + n // 2 * UP_TILE


def pack_kernel(
    route_ref, tokens_ref, gate_up_ref, out_ref, first_ref, head_ref, route, tokens, low, high, source, sem, head_sem
):
    top_count, row_count = route.shape
    chunks = tokens.shape[1] // LANES
    pitch = 2 * chunks
    peers = out_ref.shape[0] // pitch
    hidden = gate_up_ref.shape[2] // 2

    fetch_route = pltpu.make_async_copy(route_ref, route, sem.at[2])
    fetch_route.start()
    fetch = pltpu.make_async_copy(tokens_ref, tokens, sem.at[0])
    fetch.start()
    heads = []
    for n in range(HEAD):
        tile = gate_up_ref.at[0, :, pl.ds(up_start(n, hidden), UP_TILE)]
        heads.append(pltpu.make_async_copy(tile, head_ref.at[n], head_sem.at[n]))
        heads[n].start()

    low[...] = jnp.zeros_like(low)
    high[...] = jnp.zeros_like(high)
    fetch_route.wait()
    peer = lax.broadcasted_iota(jnp.int32, (top_count, peers), 1)
    lowest = jnp.full((top_count, peers), row_count, jnp.int32)
    highest = jnp.full((top_count, peers), -1, jnp.int32)
    for t in range(row_count):
        named = route[:, t : t + 1] == peer
        lowest = jnp.where(named, jnp.minimum(lowest, t), lowest)
        highest = jnp.where(named, t, highest)
    lowest = jnp.min(lowest, axis=0, keepdims=True)
    highest = jnp.max(highest, axis=0, keepdims=True)
    second = jnp.where(highest > lowest, highest, row_count)
    side = lax.broadcasted_iota(jnp.int32, (8, peers), 0)
    first_ref[...] = jnp.where(side == 0, lowest, second)
    publish = pltpu.make_async_copy(first_ref, source, sem.at[1])
    publish.start()
    fetch.wait()
    for c in range(chunks):
        part = tokens[:, c * LANES : (c + 1) * LANES].astype(F32)
        low[pl.ds(2 * c, row_count, stride=pitch), :] = part
        high[pl.ds(2 * c + 1, row_count, stride=pitch), :] = part
    publish.wait()

    def fill(i, _):
        pair = []
        for p in (2 * i, 2 * i + 1):
            a = pl.multiple_of(source[0, p] * pitch, 8)
            b = pl.multiple_of(source[1, p] * pitch, 8)
            pair.append(low[pl.ds(a, pitch), :] + high[pl.ds(b, pitch), :])
        out_ref[pl.ds(pl.multiple_of(i * 2 * pitch, 16), 2 * pitch), :] = jnp.concatenate(
            pair, axis=0
        ).astype(BF16)
        return 0

    lax.fori_loop(0, peers // 2, fill, 0, unroll=4)
    for copy in heads:
        copy.wait()


def pack(route, tokens, gate_up, peers):
    row_count, width = tokens.shape
    pitch = 2 * width // LANES
    vmem = pl.BlockSpec(memory_space=pltpu.VMEM)
    anywhere = pl.BlockSpec(memory_space=pl.ANY)
    return pl.pallas_call(
        pack_kernel,
        out_shape=(
            jax.ShapeDtypeStruct((peers * pitch, LANES), BF16),
            jax.ShapeDtypeStruct((8, peers), jnp.int32),
            jax.ShapeDtypeStruct((HEAD, width, UP_TILE), BF16),
        ),
        in_specs=[anywhere, anywhere, anywhere],
        out_specs=(vmem, vmem, vmem),
        scratch_shapes=[
            pltpu.VMEM(route.shape, jnp.int32),
            pltpu.VMEM(tokens.shape, BF16),
            pltpu.VMEM(((row_count + 1) * pitch, LANES), F32),
            pltpu.VMEM(((row_count + 1) * pitch, LANES), F32),
            pltpu.SMEM((8, peers), jnp.int32),
            pltpu.SemaphoreType.DMA((3,)),
            pltpu.SemaphoreType.DMA((HEAD,)),
        ],
        compiler_params=pltpu.CompilerParams(vmem_limit_bytes=16 * 2**20),
        name="pack",
    )(route, tokens, gate_up)


def ffn_kernel(got_ref, head_ref, gate_up_ref, down_ref, out_ref, wide, rows, gate_up, down, active, up_sem, down_sem):
    width = rows.shape[1]
    hidden = active.shape[1]
    chunks = width // LANES
    pitch = 2 * chunks
    peers = got_ref.shape[0] // pitch
    up_steps = hidden // UP_TILE
    down_steps = width // DOWN_TILE

    copies = []
    for n in range(HEAD, 2 * up_steps):
        tile = gate_up_ref.at[0, :, pl.ds(up_start(n, hidden), UP_TILE)]
        copies.append(pltpu.make_async_copy(tile, gate_up.at[n - HEAD], up_sem.at[n - HEAD]))
    for n in range(down_steps):
        copies.append(
            pltpu.make_async_copy(
                down_ref.at[0, :, pl.ds(n * DOWN_TILE, DOWN_TILE)], down.at[n], down_sem.at[n]
            )
        )
    for copy in copies[:IN_FLIGHT]:
        copy.start()

    def take(n):
        copies[n].wait()
        if n + IN_FLIGHT < len(copies):
            copies[n + IN_FLIGHT].start()

    def widen(i, _):
        span = pl.ds(pl.multiple_of(i * PIECE, PIECE), PIECE)
        wide[span, :] = got_ref[span, :].astype(F32)
        return 0

    lax.fori_loop(0, peers * pitch // PIECE, widen, 0)
    for c in range(chunks):
        for r in range(2):
            rows[r * peers : (r + 1) * peers, c * LANES : (c + 1) * LANES] = wide[
                pl.ds(2 * c + r, peers, stride=pitch), :
            ].astype(BF16)

    for step in range(up_steps):
        tiles = []
        for n in (2 * step, 2 * step + 1):
            if n >= HEAD:
                take(n - HEAD)
            tiles.append(head_ref.at[n] if n < HEAD else gate_up.at[n - HEAD])
        gate = jnp.dot(rows[...], tiles[0][...], preferred_element_type=F32)
        up = jnp.dot(rows[...], tiles[1][...], preferred_element_type=F32)
        active[:, step * UP_TILE : (step + 1) * UP_TILE] = (gate / (1 + jnp.exp(-gate)) * up).astype(BF16)

    for first in range(0, down_steps, DOWN_GROUP):
        steps = range(first, min(first + DOWN_GROUP, down_steps))
        for step in steps:
            take(2 * up_steps - HEAD + step)
        for step in steps:
            result = jnp.dot(active[...], down[step], preferred_element_type=F32)
            for q in range(DOWN_TILE // LANES):
                c = step * (DOWN_TILE // LANES) + q
                for r in range(2):
                    wide[pl.ds(2 * c + r, peers, stride=pitch), :] = result[
                        r * peers : (r + 1) * peers, q * LANES : (q + 1) * LANES
                    ]

    def narrow(i, _):
        span = pl.ds(pl.multiple_of(i * PIECE, PIECE), PIECE)
        out_ref[span, :] = wide[span, :].astype(BF16)
        return 0

    lax.fori_loop(0, peers * pitch // PIECE, narrow, 0)


def expert_ffn(got, head, gate_up, down):
    _, width, both = gate_up.shape
    hidden = both // 2
    total = got.shape[0]
    slots = total * LANES // width
    up_tiles = both // UP_TILE - HEAD
    down_tiles = width // DOWN_TILE
    return pl.pallas_call(
        ffn_kernel,
        out_shape=jax.ShapeDtypeStruct(got.shape, BF16),
        in_specs=[
            pl.BlockSpec(memory_space=pltpu.VMEM),
            pl.BlockSpec(memory_space=pltpu.VMEM),
            pl.BlockSpec(memory_space=pl.ANY),
            pl.BlockSpec(memory_space=pl.ANY),
        ],
        out_specs=pl.BlockSpec(memory_space=pltpu.VMEM),
        scratch_shapes=[
            pltpu.VMEM((total, LANES), F32),
            pltpu.VMEM((slots, width), BF16),
            pltpu.VMEM((up_tiles, width, UP_TILE), BF16),
            pltpu.VMEM((down_tiles, hidden, DOWN_TILE), BF16),
            pltpu.VMEM((slots, hidden), BF16),
            pltpu.SemaphoreType.DMA((up_tiles,)),
            pltpu.SemaphoreType.DMA((down_tiles,)),
        ],
        compiler_params=pltpu.CompilerParams(vmem_limit_bytes=44 * 2**20),
        cost_estimate=pl.CostEstimate(
            flops=2 * slots * width * hidden * 3, bytes_accessed=6 * width * hidden, transcendentals=slots * hidden
        ),
        name="expert_ffn",
    )(got, head, gate_up, down)


def combine_kernel(
    route_ref, first_ref, weight_ref, got_ref, out_ref, wide, total, narrow, scale, route, first, weight, sem
):
    top_count, row_count = route.shape
    chunks = out_ref.shape[1] // LANES
    pitch = 2 * chunks
    peers = got_ref.shape[0] // pitch

    fetch_weight = pltpu.make_async_copy(weight_ref, narrow, sem.at[0])
    fetch_route = pltpu.make_async_copy(route_ref, route, sem.at[1])
    fetch_first = pltpu.make_async_copy(first_ref, first, sem.at[2])
    fetch_weight.start()
    fetch_route.start()
    fetch_first.start()

    def widen(i, _):
        span = pl.ds(pl.multiple_of(i * PIECE, PIECE), PIECE)
        wide[span, :] = got_ref[span, :].astype(F32)
        return 0

    pieces = peers * pitch // PIECE
    lax.fori_loop(0, pieces // 2, widen, 0)
    fetch_weight.wait()
    scale[...] = narrow[...].astype(F32)
    publish = pltpu.make_async_copy(scale, weight, sem.at[3])
    publish.start()
    lax.fori_loop(pieces // 2, pieces, widen, 0)
    fetch_route.wait()
    fetch_first.wait()
    publish.wait()
    parity = lax.broadcasted_iota(jnp.int32, (8, LANES), 0) % 2

    def add_up(t, _):
        acc = jnp.zeros((pitch // 8, 8, LANES), F32)
        for k in range(top_count):
            e = route[k, t]
            start = pl.multiple_of(e * pitch, 8)
            rank = jnp.where(first[0, e] == t, 0, 1)
            factor = jnp.where(parity == rank, weight[k, t], 0.0)
            acc += wide[pl.ds(start, pitch), :].reshape(pitch // 8, 8, LANES) * factor[None]
        total[pl.ds(pl.multiple_of(t * pitch, 8), pitch), :] = acc.reshape(pitch, LANES)
        return 0

    lax.fori_loop(0, row_count, add_up, 0, unroll=4)
    for c in range(chunks):
        out_ref[:, c * LANES : (c + 1) * LANES] = (
            total[pl.ds(2 * c, row_count, stride=pitch), :] + total[pl.ds(2 * c + 1, row_count, stride=pitch), :]
        ).astype(BF16)


def combine(route, first, weight, got, width):
    row_count = route.shape[1]
    pitch = 2 * width // LANES
    anywhere = pl.BlockSpec(memory_space=pl.ANY)
    vmem = pl.BlockSpec(memory_space=pltpu.VMEM)
    return pl.pallas_call(
        combine_kernel,
        out_shape=jax.ShapeDtypeStruct((row_count, width), BF16),
        in_specs=[anywhere, anywhere, anywhere, vmem],
        out_specs=vmem,
        scratch_shapes=[
            pltpu.VMEM(got.shape, F32),
            pltpu.VMEM((row_count * pitch, LANES), F32),
            pltpu.VMEM(weight.shape, BF16),
            pltpu.VMEM(weight.shape, F32),
            pltpu.SMEM(route.shape, jnp.int32),
            pltpu.SMEM(first.shape, jnp.int32),
            pltpu.SMEM(weight.shape, F32),
            pltpu.SemaphoreType.DMA((4,)),
        ],
        compiler_params=pltpu.CompilerParams(vmem_limit_bytes=24 * 2**20),
        name="combine",
    )(route, first, weight, got)


def stay_in_hbm(array):
    return pltpu.with_memory_space_constraint(array, pltpu.HBM)


def exchange(blocks, peers):
    shape = blocks.shape
    blocks = blocks.reshape(peers, -1, LANES)
    return lax.all_to_all(blocks, ("node", "local"), split_axis=0, concat_axis=0, tiled=True).reshape(shape)


def on_device(tokens, route, combine_weight, gate_up, down):
    width = tokens.shape[1]
    peers = lax.axis_size("node") * lax.axis_size("local")
    route = route.T
    send, first, head = pack(
        stay_in_hbm(route),
        stay_in_hbm(tokens),
        stay_in_hbm(gate_up),
        peers,
    )
    got = exchange(send, peers)
    result = expert_ffn(got, head, stay_in_hbm(gate_up), stay_in_hbm(down))
    back = exchange(result, peers)
    return combine(route, first, combine_weight.T, back, width)


def solution(mesh):
    spec = P(("node", "local"), None)
    weights = P(("node", "local"), None, None)
    return jax.shard_map(
        on_device,
        mesh=mesh,
        in_specs=(spec, spec, spec, weights, weights),
        out_specs=spec,
        check_vma=False,
    )
```

```python
import jax
import jax.numpy as jnp
from jax import lax
from jax.experimental import pallas as pl
from jax.experimental.pallas import tpu as pltpu
from jax.sharding import PartitionSpec as P

LANES = 128
F32 = jnp.float32
BF16 = jnp.bfloat16
UP_TILE = 256
HEAD = 2
DOWN_TILE = 512
PIECE = 512


def up_start(n, hidden):
    return n % 2 * hidden + n // 2 * UP_TILE


def pack_kernel(
    route_ref, tokens_ref, gate_up_ref, out_ref, first_ref, head_ref, route, tokens, low, high, source, sem, head_sem
):
    top_count, row_count = route.shape
    chunks = tokens.shape[1] // LANES
    pitch = 2 * chunks
    peers = out_ref.shape[0] // pitch
    hidden = gate_up_ref.shape[2] // 2

    fetch_route = pltpu.make_async_copy(route_ref, route, sem.at[2])
    fetch_route.start()
    fetch = pltpu.make_async_copy(tokens_ref, tokens, sem.at[0])
    fetch.start()
    heads = []
    for n in range(HEAD):
        tile = gate_up_ref.at[0, :, pl.ds(up_start(n, hidden), UP_TILE)]
        heads.append(pltpu.make_async_copy(tile, head_ref.at[n], head_sem.at[n]))
        heads[n].start()

    low[...] = jnp.zeros_like(low)
    high[...] = jnp.zeros_like(high)
    fetch_route.wait()
    peer = lax.broadcasted_iota(jnp.int32, (top_count, peers), 1)
    lowest = jnp.full((top_count, peers), row_count, jnp.int32)
    highest = jnp.full((top_count, peers), -1, jnp.int32)
    for t in range(row_count):
        named = route[:, t : t + 1] == peer
        lowest = jnp.where(named, jnp.minimum(lowest, t), lowest)
        highest = jnp.where(named, t, highest)
    lowest = jnp.min(lowest, axis=0, keepdims=True)
    highest = jnp.max(highest, axis=0, keepdims=True)
    second = jnp.where(highest > lowest, highest, row_count)
    side = lax.broadcasted_iota(jnp.int32, (8, peers), 0)
    first_ref[...] = jnp.where(side == 0, lowest, second)
    publish = pltpu.make_async_copy(first_ref, source, sem.at[1])
    publish.start()
    fetch.wait()
    for c in range(chunks):
        part = tokens[:, c * LANES : (c + 1) * LANES].astype(F32)
        low[pl.ds(2 * c, row_count, stride=pitch), :] = part
        high[pl.ds(2 * c + 1, row_count, stride=pitch), :] = part
    publish.wait()

    def fill(i, _):
        pair = []
        for p in (2 * i, 2 * i + 1):
            a = pl.multiple_of(source[0, p] * pitch, 8)
            b = pl.multiple_of(source[1, p] * pitch, 8)
            pair.append(low[pl.ds(a, pitch), :] + high[pl.ds(b, pitch), :])
        out_ref[pl.ds(pl.multiple_of(i * 2 * pitch, 16), 2 * pitch), :] = jnp.concatenate(
            pair, axis=0
        ).astype(BF16)
        return 0

    lax.fori_loop(0, peers // 2, fill, 0, unroll=4)
    for copy in heads:
        copy.wait()


def pack(route, tokens, gate_up, peers):
    row_count, width = tokens.shape
    pitch = 2 * width // LANES
    vmem = pl.BlockSpec(memory_space=pltpu.VMEM)
    anywhere = pl.BlockSpec(memory_space=pl.ANY)
    return pl.pallas_call(
        pack_kernel,
        out_shape=(
            jax.ShapeDtypeStruct((peers * pitch, LANES), BF16),
            jax.ShapeDtypeStruct((8, peers), jnp.int32),
            jax.ShapeDtypeStruct((HEAD, width, UP_TILE), BF16),
        ),
        in_specs=[anywhere, anywhere, anywhere],
        out_specs=(vmem, vmem, vmem),
        scratch_shapes=[
            pltpu.VMEM(route.shape, jnp.int32),
            pltpu.VMEM(tokens.shape, BF16),
            pltpu.VMEM(((row_count + 1) * pitch, LANES), F32),
            pltpu.VMEM(((row_count + 1) * pitch, LANES), F32),
            pltpu.SMEM((8, peers), jnp.int32),
            pltpu.SemaphoreType.DMA((3,)),
            pltpu.SemaphoreType.DMA((HEAD,)),
        ],
        compiler_params=pltpu.CompilerParams(vmem_limit_bytes=16 * 2**20),
        name="pack",
    )(route, tokens, gate_up)


def ffn_kernel(got_ref, head_ref, gate_up_ref, down_ref, out_ref, wide, rows, gate_up, active, up_sem):
    width = rows.shape[1]
    hidden = active.shape[1]
    chunks = width // LANES
    pitch = 2 * chunks
    peers = got_ref.shape[0] // pitch
    up_steps = hidden // UP_TILE

    copies = []
    for n in range(HEAD, 2 * up_steps):
        tile = gate_up_ref.at[0, :, pl.ds(up_start(n, hidden), UP_TILE)]
        copies.append(pltpu.make_async_copy(tile, gate_up.at[n - HEAD], up_sem.at[n - HEAD]))
    for copy in copies[:2]:
        copy.start()

    for copy in copies[2:]:
        copy.start(priority=1)

    def widen(i, _):
        span = pl.ds(pl.multiple_of(i * PIECE, PIECE), PIECE)
        wide[span, :] = got_ref[span, :].astype(F32)
        return 0

    lax.fori_loop(0, peers * pitch // PIECE, widen, 0)
    for c in range(chunks):
        for r in range(2):
            rows[r * peers : (r + 1) * peers, c * LANES : (c + 1) * LANES] = wide[
                pl.ds(2 * c + r, peers, stride=pitch), :
            ].astype(BF16)

    for step in range(up_steps):
        tiles = []
        for n in (2 * step, 2 * step + 1):
            if n >= HEAD:
                copies[n - HEAD].wait()
            tiles.append(head_ref.at[n] if n < HEAD else gate_up.at[n - HEAD])
        gate = jnp.dot(rows[...], tiles[0][...], preferred_element_type=F32)
        up = jnp.dot(rows[...], tiles[1][...], preferred_element_type=F32)
        active[:, step * UP_TILE : (step + 1) * UP_TILE] = (gate / (1 + jnp.exp(-gate)) * up).astype(BF16)

    for n in range(0, width, DOWN_TILE):
        result = jnp.dot(active[...], down_ref[0, :, n : n + DOWN_TILE], preferred_element_type=F32)
        for q in range(0, DOWN_TILE, LANES):
            for r in range(2):
                wide[pl.ds(2 * (n + q) // LANES + r, peers, stride=pitch), :] = result[
                    r * peers : (r + 1) * peers, q : q + LANES
                ]

    def narrow(i, _):
        span = pl.ds(pl.multiple_of(i * PIECE, PIECE), PIECE)
        out_ref[span, :] = wide[span, :].astype(BF16)
        return 0

    lax.fori_loop(0, peers * pitch // PIECE, narrow, 0)


def expert_ffn(got, head, gate_up, down):
    _, width, both = gate_up.shape
    hidden = both // 2
    total = got.shape[0]
    slots = total * LANES // width
    up_tiles = both // UP_TILE - HEAD
    vmem = pl.BlockSpec(memory_space=pltpu.VMEM)
    return pl.pallas_call(
        ffn_kernel,
        out_shape=jax.ShapeDtypeStruct(got.shape, BF16),
        in_specs=[vmem, vmem, pl.BlockSpec(memory_space=pl.ANY), vmem],
        out_specs=vmem,
        scratch_shapes=[
            pltpu.VMEM((total, LANES), F32),
            pltpu.VMEM((slots, width), BF16),
            pltpu.VMEM((up_tiles, width, UP_TILE), BF16),
            pltpu.VMEM((slots, hidden), BF16),
            pltpu.SemaphoreType.DMA((up_tiles,)),
        ],
        compiler_params=pltpu.CompilerParams(vmem_limit_bytes=30 * 2**20),
        cost_estimate=pl.CostEstimate(
            flops=2 * slots * width * hidden * 3, bytes_accessed=6 * width * hidden, transcendentals=slots * hidden
        ),
        name="expert_ffn",
    )(got, head, gate_up, down)


def combine_kernel(
    route_ref, first_ref, weight_ref, got_ref, out_ref, wide, total, narrow, scale, route, first, weight, sem
):
    top_count, row_count = route.shape
    chunks = out_ref.shape[1] // LANES
    pitch = 2 * chunks
    peers = got_ref.shape[0] // pitch

    fetch_weight = pltpu.make_async_copy(weight_ref, narrow, sem.at[0])
    fetch_route = pltpu.make_async_copy(route_ref, route, sem.at[1])
    fetch_first = pltpu.make_async_copy(first_ref, first, sem.at[2])
    fetch_weight.start()
    fetch_route.start()
    fetch_first.start()

    def widen(i, _):
        span = pl.ds(pl.multiple_of(i * PIECE, PIECE), PIECE)
        wide[span, :] = got_ref[span, :].astype(F32)
        return 0

    pieces = peers * pitch // PIECE
    lax.fori_loop(0, pieces // 2, widen, 0)
    fetch_weight.wait()
    scale[...] = narrow[...].astype(F32)
    publish = pltpu.make_async_copy(scale, weight, sem.at[3])
    publish.start()
    lax.fori_loop(pieces // 2, pieces, widen, 0)
    fetch_route.wait()
    fetch_first.wait()
    publish.wait()
    parity = lax.broadcasted_iota(jnp.int32, (8, LANES), 0) % 2

    def add_up(t, _):
        acc = jnp.zeros((pitch // 8, 8, LANES), F32)
        for k in range(top_count):
            e = route[k, t]
            start = pl.multiple_of(e * pitch, 8)
            rank = jnp.where(first[0, e] == t, 0, 1)
            factor = jnp.where(parity == rank, weight[k, t], 0.0)
            acc += wide[pl.ds(start, pitch), :].reshape(pitch // 8, 8, LANES) * factor[None]
        total[pl.ds(pl.multiple_of(t * pitch, 8), pitch), :] = acc.reshape(pitch, LANES)
        return 0

    lax.fori_loop(0, row_count, add_up, 0, unroll=4)
    for c in range(chunks):
        out_ref[:, c * LANES : (c + 1) * LANES] = (
            total[pl.ds(2 * c, row_count, stride=pitch), :] + total[pl.ds(2 * c + 1, row_count, stride=pitch), :]
        ).astype(BF16)


def combine(route, first, weight, got, width):
    row_count = route.shape[1]
    pitch = 2 * width // LANES
    anywhere = pl.BlockSpec(memory_space=pl.ANY)
    vmem = pl.BlockSpec(memory_space=pltpu.VMEM)
    return pl.pallas_call(
        combine_kernel,
        out_shape=jax.ShapeDtypeStruct((row_count, width), BF16),
        in_specs=[anywhere, anywhere, anywhere, vmem],
        out_specs=vmem,
        scratch_shapes=[
            pltpu.VMEM(got.shape, F32),
            pltpu.VMEM((row_count * pitch, LANES), F32),
            pltpu.VMEM(weight.shape, BF16),
            pltpu.VMEM(weight.shape, F32),
            pltpu.SMEM(route.shape, jnp.int32),
            pltpu.SMEM(first.shape, jnp.int32),
            pltpu.SMEM(weight.shape, F32),
            pltpu.SemaphoreType.DMA((4,)),
        ],
        compiler_params=pltpu.CompilerParams(vmem_limit_bytes=24 * 2**20),
        name="combine",
    )(route, first, weight, got)


def stay_in_hbm(array):
    return pltpu.with_memory_space_constraint(array, pltpu.HBM)


def exchange(blocks, peers):
    shape = blocks.shape
    blocks = blocks.reshape(peers, -1, LANES)
    return lax.all_to_all(blocks, ("node", "local"), split_axis=0, concat_axis=0, tiled=True).reshape(shape)


def on_device(tokens, route, combine_weight, gate_up, down):
    width = tokens.shape[1]
    peers = lax.axis_size("node") * lax.axis_size("local")
    route = route.T
    send, first, head = pack(
        stay_in_hbm(route),
        stay_in_hbm(tokens),
        stay_in_hbm(gate_up),
        peers,
    )
    got = exchange(send, peers)
    result = expert_ffn(got, head, stay_in_hbm(gate_up), down)
    back = exchange(result, peers)
    return combine(route, first, combine_weight.T, back, width)


def solution(mesh):
    spec = P(("node", "local"), None)
    weights = P(("node", "local"), None, None)
    return jax.shard_map(
        on_device,
        mesh=mesh,
        in_specs=(spec, spec, spec, weights, weights),
        out_specs=spec,
        check_vma=False,
    )
```

```python
import jax
import jax.numpy as jnp
from jax import lax
from jax.experimental import pallas as pl
from jax.experimental.pallas import tpu as pltpu
from jax.sharding import PartitionSpec as P

LANES = 128
F32 = jnp.float32
BF16 = jnp.bfloat16
UP_TILE = 256
DOWN_TILE = 512
PIECE = 512


def pack_kernel(
    route_ref, tokens_ref, out_ref, first_ref, route, tokens, low, high, source, sem
):
    top_count, row_count = route.shape
    chunks = tokens.shape[1] // LANES
    pitch = 2 * chunks
    peers = out_ref.shape[0] // pitch

    fetch_route = pltpu.make_async_copy(route_ref, route, sem.at[2])
    fetch_route.start()
    fetch = pltpu.make_async_copy(tokens_ref, tokens, sem.at[0])
    fetch.start()
    low[...] = jnp.zeros_like(low)
    high[...] = jnp.zeros_like(high)
    fetch_route.wait()
    peer = lax.broadcasted_iota(jnp.int32, (top_count, peers), 1)
    lowest = jnp.full((top_count, peers), row_count, jnp.int32)
    highest = jnp.full((top_count, peers), -1, jnp.int32)
    for t in range(row_count):
        named = route[:, t : t + 1] == peer
        lowest = jnp.where(named, jnp.minimum(lowest, t), lowest)
        highest = jnp.where(named, t, highest)
    lowest = jnp.min(lowest, axis=0, keepdims=True)
    highest = jnp.max(highest, axis=0, keepdims=True)
    second = jnp.where(highest > lowest, highest, row_count)
    side = lax.broadcasted_iota(jnp.int32, (8, peers), 0)
    first_ref[...] = jnp.where(side == 0, lowest, second)
    publish = pltpu.make_async_copy(first_ref, source, sem.at[1])
    publish.start()
    fetch.wait()
    for c in range(chunks):
        part = tokens[:, c * LANES : (c + 1) * LANES].astype(F32)
        low[pl.ds(2 * c, row_count, stride=pitch), :] = part
        high[pl.ds(2 * c + 1, row_count, stride=pitch), :] = part
    publish.wait()

    def fill(i, _):
        pair = []
        for p in (2 * i, 2 * i + 1):
            a = pl.multiple_of(source[0, p] * pitch, 8)
            b = pl.multiple_of(source[1, p] * pitch, 8)
            pair.append(low[pl.ds(a, pitch), :] + high[pl.ds(b, pitch), :])
        out_ref[pl.ds(pl.multiple_of(i * 2 * pitch, 16), 2 * pitch), :] = jnp.concatenate(
            pair, axis=0
        ).astype(BF16)
        return 0

    lax.fori_loop(0, peers // 2, fill, 0, unroll=4)


def pack(route, tokens, peers):
    row_count, width = tokens.shape
    pitch = 2 * width // LANES
    vmem = pl.BlockSpec(memory_space=pltpu.VMEM)
    anywhere = pl.BlockSpec(memory_space=pl.ANY)
    return pl.pallas_call(
        pack_kernel,
        out_shape=(
            jax.ShapeDtypeStruct((peers * pitch, LANES), BF16),
            jax.ShapeDtypeStruct((8, peers), jnp.int32),
        ),
        in_specs=[anywhere, anywhere],
        out_specs=(vmem, vmem),
        scratch_shapes=[
            pltpu.VMEM(route.shape, jnp.int32),
            pltpu.VMEM(tokens.shape, BF16),
            pltpu.VMEM(((row_count + 1) * pitch, LANES), F32),
            pltpu.VMEM(((row_count + 1) * pitch, LANES), F32),
            pltpu.SMEM((8, peers), jnp.int32),
            pltpu.SemaphoreType.DMA((3,)),
        ],
        compiler_params=pltpu.CompilerParams(vmem_limit_bytes=16 * 2**20),
        cost_estimate=pl.CostEstimate(flops=20000000000, bytes_accessed=1000, transcendentals=0),
        name="pack",
    )(route, tokens)


def ffn_kernel(got_ref, gate_up_ref, down_ref, out_ref, wide, rows, active):
    width = rows.shape[1]
    hidden = active.shape[1]
    chunks = width // LANES
    pitch = 2 * chunks
    peers = got_ref.shape[0] // pitch

    def widen(i, _):
        span = pl.ds(pl.multiple_of(i * PIECE, PIECE), PIECE)
        wide[span, :] = got_ref[span, :].astype(F32)
        return 0

    lax.fori_loop(0, peers * pitch // PIECE, widen, 0)
    for c in range(chunks):
        for r in range(2):
            rows[r * peers : (r + 1) * peers, c * LANES : (c + 1) * LANES] = wide[
                pl.ds(2 * c + r, peers, stride=pitch), :
            ].astype(BF16)

    for n in range(0, hidden, UP_TILE):
        gate = jnp.dot(rows[...], gate_up_ref[0, :, n : n + UP_TILE], preferred_element_type=F32)
        up = jnp.dot(rows[...], gate_up_ref[0, :, hidden + n : hidden + n + UP_TILE], preferred_element_type=F32)
        active[:, n : n + UP_TILE] = (gate / (1 + jnp.exp(-gate)) * up).astype(BF16)

    for n in range(0, width, DOWN_TILE):
        result = jnp.dot(active[...], down_ref[0, :, n : n + DOWN_TILE], preferred_element_type=F32)
        for q in range(0, DOWN_TILE, LANES):
            for r in range(2):
                wide[pl.ds(2 * (n + q) // LANES + r, peers, stride=pitch), :] = result[
                    r * peers : (r + 1) * peers, q : q + LANES
                ]

    def narrow(i, _):
        span = pl.ds(pl.multiple_of(i * PIECE, PIECE), PIECE)
        out_ref[span, :] = wide[span, :].astype(BF16)
        return 0

    lax.fori_loop(0, peers * pitch // PIECE, narrow, 0)


def expert_ffn(got, gate_up, down):
    _, width, both = gate_up.shape
    hidden = both // 2
    total = got.shape[0]
    slots = total * LANES // width
    return pl.pallas_call(
        ffn_kernel,
        out_shape=jax.ShapeDtypeStruct(got.shape, BF16),
        in_specs=[pl.BlockSpec(memory_space=pltpu.VMEM)] * 3,
        out_specs=pl.BlockSpec(memory_space=pltpu.VMEM),
        scratch_shapes=[
            pltpu.VMEM((total, LANES), F32),
            pltpu.VMEM((slots, width), BF16),
            pltpu.VMEM((slots, hidden), BF16),
        ],
        compiler_params=pltpu.CompilerParams(vmem_limit_bytes=12 * 2**20),
        cost_estimate=pl.CostEstimate(
            flops=2 * slots * width * hidden * 3, bytes_accessed=6 * width * hidden, transcendentals=slots * hidden
        ),
        name="expert_ffn",
    )(got, gate_up, down)


def combine_kernel(
    route_ref, first_ref, weight_ref, got_ref, out_ref, wide, total, narrow, scale, route, first, weight, sem
):
    top_count, row_count = route.shape
    chunks = out_ref.shape[1] // LANES
    pitch = 2 * chunks
    peers = got_ref.shape[0] // pitch

    fetch_weight = pltpu.make_async_copy(weight_ref, narrow, sem.at[0])
    fetch_route = pltpu.make_async_copy(route_ref, route, sem.at[1])
    fetch_first = pltpu.make_async_copy(first_ref, first, sem.at[2])
    fetch_weight.start()
    fetch_route.start()
    fetch_first.start()

    def widen(i, _):
        span = pl.ds(pl.multiple_of(i * PIECE, PIECE), PIECE)
        wide[span, :] = got_ref[span, :].astype(F32)
        return 0

    pieces = peers * pitch // PIECE
    lax.fori_loop(0, pieces // 2, widen, 0)
    fetch_weight.wait()
    scale[...] = narrow[...].astype(F32)
    publish = pltpu.make_async_copy(scale, weight, sem.at[3])
    publish.start()
    lax.fori_loop(pieces // 2, pieces, widen, 0)
    fetch_route.wait()
    fetch_first.wait()
    publish.wait()
    parity = lax.broadcasted_iota(jnp.int32, (8, LANES), 0) % 2

    def add_up(t, _):
        acc = jnp.zeros((pitch // 8, 8, LANES), F32)
        for k in range(top_count):
            e = route[k, t]
            start = pl.multiple_of(e * pitch, 8)
            rank = jnp.where(first[0, e] == t, 0, 1)
            factor = jnp.where(parity == rank, weight[k, t], 0.0)
            acc += wide[pl.ds(start, pitch), :].reshape(pitch // 8, 8, LANES) * factor[None]
        total[pl.ds(pl.multiple_of(t * pitch, 8), pitch), :] = acc.reshape(pitch, LANES)
        return 0

    lax.fori_loop(0, row_count, add_up, 0, unroll=4)
    for c in range(chunks):
        out_ref[:, c * LANES : (c + 1) * LANES] = (
            total[pl.ds(2 * c, row_count, stride=pitch), :] + total[pl.ds(2 * c + 1, row_count, stride=pitch), :]
        ).astype(BF16)


def combine(route, first, weight, got, width):
    row_count = route.shape[1]
    pitch = 2 * width // LANES
    anywhere = pl.BlockSpec(memory_space=pl.ANY)
    vmem = pl.BlockSpec(memory_space=pltpu.VMEM)
    return pl.pallas_call(
        combine_kernel,
        out_shape=jax.ShapeDtypeStruct((row_count, width), BF16),
        in_specs=[anywhere, anywhere, anywhere, vmem],
        out_specs=vmem,
        scratch_shapes=[
            pltpu.VMEM(got.shape, F32),
            pltpu.VMEM((row_count * pitch, LANES), F32),
            pltpu.VMEM(weight.shape, BF16),
            pltpu.VMEM(weight.shape, F32),
            pltpu.SMEM(route.shape, jnp.int32),
            pltpu.SMEM(first.shape, jnp.int32),
            pltpu.SMEM(weight.shape, F32),
            pltpu.SemaphoreType.DMA((4,)),
        ],
        compiler_params=pltpu.CompilerParams(vmem_limit_bytes=24 * 2**20),
        name="combine",
    )(route, first, weight, got)


def stay_in_hbm(array):
    return pltpu.with_memory_space_constraint(array, pltpu.HBM)


def exchange(blocks, peers):
    shape = blocks.shape
    blocks = blocks.reshape(peers, -1, LANES)
    return lax.all_to_all(blocks, ("node", "local"), split_axis=0, concat_axis=0, tiled=True).reshape(shape)


def on_device(tokens, route, combine_weight, gate_up, down):
    width = tokens.shape[1]
    peers = lax.axis_size("node") * lax.axis_size("local")
    route = route.T
    send, first = pack(stay_in_hbm(route), stay_in_hbm(tokens), peers)
    got = exchange(send, peers)
    result = expert_ffn(got, gate_up, down)
    back = exchange(result, peers)
    return combine(route, first, combine_weight.T, back, width)


def solution(mesh):
    spec = P(("node", "local"), None)
    weights = P(("node", "local"), None, None)
    return jax.shard_map(
        on_device,
        mesh=mesh,
        in_specs=(spec, spec, spec, weights, weights),
        out_specs=spec,
        check_vma=False,
    )
```

```python
import jax
import jax.numpy as jnp
from jax import lax
from jax.experimental import pallas as pl
from jax.experimental.pallas import tpu as pltpu
from jax.sharding import PartitionSpec as P

LANES = 128
F32 = jnp.float32
BF16 = jnp.bfloat16
UP_TILE = 512
DEPTH_TILE = 512
DOWN_TILE = 512
PIECE = 512


def pack_kernel(
    route_ref, tokens_ref, out_ref, first_ref, route, tokens, low, high, source, sem
):
    top_count, row_count = route.shape
    chunks = tokens.shape[1] // LANES
    pitch = 2 * chunks
    peers = out_ref.shape[0] // pitch

    fetch_route = pltpu.make_async_copy(route_ref, route, sem.at[2])
    fetch_route.start()
    fetch = pltpu.make_async_copy(tokens_ref, tokens, sem.at[0])
    fetch.start()
    low[...] = jnp.zeros_like(low)
    high[...] = jnp.zeros_like(high)
    fetch_route.wait()
    peer = lax.broadcasted_iota(jnp.int32, (top_count, peers), 1)
    lowest = jnp.full((top_count, peers), row_count, jnp.int32)
    highest = jnp.full((top_count, peers), -1, jnp.int32)
    for t in range(row_count):
        named = route[:, t : t + 1] == peer
        lowest = jnp.where(named, jnp.minimum(lowest, t), lowest)
        highest = jnp.where(named, t, highest)
    lowest = jnp.min(lowest, axis=0, keepdims=True)
    highest = jnp.max(highest, axis=0, keepdims=True)
    second = jnp.where(highest > lowest, highest, row_count)
    side = lax.broadcasted_iota(jnp.int32, (8, peers), 0)
    first_ref[...] = jnp.where(side == 0, lowest, second)
    publish = pltpu.make_async_copy(first_ref, source, sem.at[1])
    publish.start()
    fetch.wait()
    for c in range(chunks):
        part = tokens[:, c * LANES : (c + 1) * LANES].astype(F32)
        low[pl.ds(2 * c, row_count, stride=pitch), :] = part
        high[pl.ds(2 * c + 1, row_count, stride=pitch), :] = part
    publish.wait()

    def fill(i, _):
        pair = []
        for p in (2 * i, 2 * i + 1):
            a = pl.multiple_of(source[0, p] * pitch, 8)
            b = pl.multiple_of(source[1, p] * pitch, 8)
            pair.append(low[pl.ds(a, pitch), :] + high[pl.ds(b, pitch), :])
        out_ref[pl.ds(pl.multiple_of(i * 2 * pitch, 16), 2 * pitch), :] = jnp.concatenate(
            pair, axis=0
        ).astype(BF16)
        return 0

    lax.fori_loop(0, peers // 2, fill, 0, unroll=4)


def pack(route, tokens, peers):
    row_count, width = tokens.shape
    pitch = 2 * width // LANES
    vmem = pl.BlockSpec(memory_space=pltpu.VMEM)
    anywhere = pl.BlockSpec(memory_space=pl.ANY)
    return pl.pallas_call(
        pack_kernel,
        out_shape=(
            jax.ShapeDtypeStruct((peers * pitch, LANES), BF16),
            jax.ShapeDtypeStruct((8, peers), jnp.int32),
        ),
        in_specs=[anywhere, anywhere],
        out_specs=(vmem, vmem),
        scratch_shapes=[
            pltpu.VMEM(route.shape, jnp.int32),
            pltpu.VMEM(tokens.shape, BF16),
            pltpu.VMEM(((row_count + 1) * pitch, LANES), F32),
            pltpu.VMEM(((row_count + 1) * pitch, LANES), F32),
            pltpu.SMEM((8, peers), jnp.int32),
            pltpu.SemaphoreType.DMA((3,)),
        ],
        compiler_params=pltpu.CompilerParams(vmem_limit_bytes=16 * 2**20),
        cost_estimate=pl.CostEstimate(flops=20_000_000_000, bytes_accessed=1000, transcendentals=0),
        name="pack",
    )(route, tokens)


def ffn_kernel(got_ref, gate_up_ref, down_ref, out_ref, wide, rows, active):
    width = rows.shape[1]
    hidden = active.shape[1]
    chunks = width // LANES
    pitch = 2 * chunks
    peers = got_ref.shape[0] // pitch

    def widen(i, _):
        span = pl.ds(pl.multiple_of(i * PIECE, PIECE), PIECE)
        wide[span, :] = got_ref[span, :].astype(F32)
        return 0

    lax.fori_loop(0, peers * pitch // PIECE, widen, 0)
    def build(depth):
        for c in range(depth // LANES, (depth + DEPTH_TILE) // LANES):
            for r in range(2):
                rows[r * peers : (r + 1) * peers, c * LANES : (c + 1) * LANES] = wide[
                    pl.ds(2 * c + r, peers, stride=pitch), :
                ].astype(BF16)

    for n in range(0, hidden, UP_TILE):
        if n == 0:
            gate = up = 0
            for depth in range(0, width, DEPTH_TILE):
                build(depth)
                span = slice(depth, depth + DEPTH_TILE)
                gate += jnp.dot(rows[:, span], gate_up_ref[0, span, :UP_TILE], preferred_element_type=F32)
                up += jnp.dot(
                    rows[:, span], gate_up_ref[0, span, hidden : hidden + UP_TILE], preferred_element_type=F32
                )
        else:
            gate = jnp.dot(rows[...], gate_up_ref[0, :, n : n + UP_TILE], preferred_element_type=F32)
            up = jnp.dot(rows[...], gate_up_ref[0, :, hidden + n : hidden + n + UP_TILE], preferred_element_type=F32)
        active[:, n : n + UP_TILE] = (gate / (1 + jnp.exp(-gate)) * up).astype(BF16)

    for n in range(0, width, DOWN_TILE):
        result = jnp.dot(active[...], down_ref[0, :, n : n + DOWN_TILE], preferred_element_type=F32)
        for q in range(0, DOWN_TILE, LANES):
            for r in range(2):
                wide[pl.ds(2 * (n + q) // LANES + r, peers, stride=pitch), :] = result[
                    r * peers : (r + 1) * peers, q : q + LANES
                ]

    def narrow(i, _):
        span = pl.ds(pl.multiple_of(i * PIECE, PIECE), PIECE)
        out_ref[span, :] = wide[span, :].astype(BF16)
        return 0

    lax.fori_loop(0, peers * pitch // PIECE, narrow, 0)


def expert_ffn(got, gate_up, down):
    _, width, both = gate_up.shape
    hidden = both // 2
    total = got.shape[0]
    slots = total * LANES // width
    return pl.pallas_call(
        ffn_kernel,
        out_shape=jax.ShapeDtypeStruct(got.shape, BF16),
        in_specs=[pl.BlockSpec(memory_space=pltpu.VMEM)] * 3,
        out_specs=pl.BlockSpec(memory_space=pltpu.VMEM),
        scratch_shapes=[
            pltpu.VMEM((total, LANES), F32),
            pltpu.VMEM((slots, width), BF16),
            pltpu.VMEM((slots, hidden), BF16),
        ],
        compiler_params=pltpu.CompilerParams(vmem_limit_bytes=12 * 2**20),
        cost_estimate=pl.CostEstimate(
            flops=2 * slots * width * hidden * 3, bytes_accessed=6 * width * hidden, transcendentals=slots * hidden
        ),
        name="expert_ffn",
    )(got, gate_up, down)


def combine_kernel(
    route_ref, first_ref, weight_ref, got_ref, out_ref, wide, total, scale, route, first, weight, sem
):
    top_count, row_count = route.shape
    chunks = out_ref.shape[1] // LANES
    pitch = 2 * chunks
    peers = got_ref.shape[0] // pitch

    fetch_route = pltpu.make_async_copy(route_ref, route, sem.at[0])
    fetch_first = pltpu.make_async_copy(first_ref, first, sem.at[1])
    fetch_route.start()
    fetch_first.start()
    scale[...] = weight_ref[...].astype(F32)
    publish = pltpu.make_async_copy(scale, weight, sem.at[2])
    publish.start()

    def widen(i, _):
        span = pl.ds(pl.multiple_of(i * PIECE, PIECE), PIECE)
        wide[span, :] = got_ref[span, :].astype(F32)
        return 0

    lax.fori_loop(0, peers * pitch // PIECE, widen, 0)
    fetch_route.wait()
    fetch_first.wait()
    publish.wait()
    parity = lax.broadcasted_iota(jnp.int32, (8, LANES), 0) % 2

    def add_up(t, _):
        acc = jnp.zeros((pitch // 8, 8, LANES), F32)
        for k in range(top_count):
            e = route[k, t]
            start = pl.multiple_of(e * pitch, 8)
            rank = jnp.where(first[0, e] == t, 0, 1)
            factor = jnp.where(parity == rank, weight[k, t], 0.0)
            acc += wide[pl.ds(start, pitch), :].reshape(pitch // 8, 8, LANES) * factor[None]
        total[pl.ds(pl.multiple_of(t * pitch, 8), pitch), :] = acc.reshape(pitch, LANES)
        return 0

    lax.fori_loop(0, row_count, add_up, 0, unroll=4)
    for c in range(chunks):
        out_ref[:, c * LANES : (c + 1) * LANES] = (
            total[pl.ds(2 * c, row_count, stride=pitch), :] + total[pl.ds(2 * c + 1, row_count, stride=pitch), :]
        ).astype(BF16)


def combine(route, first, weight, got, width):
    row_count = route.shape[1]
    pitch = 2 * width // LANES
    anywhere = pl.BlockSpec(memory_space=pl.ANY)
    vmem = pl.BlockSpec(memory_space=pltpu.VMEM)
    return pl.pallas_call(
        combine_kernel,
        out_shape=jax.ShapeDtypeStruct((row_count, width), BF16),
        in_specs=[anywhere, anywhere, vmem, vmem],
        out_specs=vmem,
        scratch_shapes=[
            pltpu.VMEM(got.shape, F32),
            pltpu.VMEM((row_count * pitch, LANES), F32),
            pltpu.VMEM(weight.shape, F32),
            pltpu.SMEM(route.shape, jnp.int32),
            pltpu.SMEM(first.shape, jnp.int32),
            pltpu.SMEM(weight.shape, F32),
            pltpu.SemaphoreType.DMA((3,)),
        ],
        compiler_params=pltpu.CompilerParams(vmem_limit_bytes=24 * 2**20),
        name="combine",
    )(route, first, weight, got)


def stay_in_hbm(array):
    return pltpu.with_memory_space_constraint(array, pltpu.HBM)


def exchange(blocks, peers):
    shape = blocks.shape
    blocks = blocks.reshape(peers, -1, LANES)
    return lax.all_to_all(blocks, ("node", "local"), split_axis=0, concat_axis=0, tiled=True).reshape(shape)


def on_device(tokens, route, combine_weight, gate_up, down):
    width = tokens.shape[1]
    peers = lax.axis_size("node") * lax.axis_size("local")
    route = route.T
    send, first = pack(stay_in_hbm(route), stay_in_hbm(tokens), peers)
    got = exchange(send, peers)
    result = expert_ffn(got, gate_up, down)
    back = exchange(result, peers)
    return combine(route, first, combine_weight.T, back, width)


def solution(mesh):
    spec = P(("node", "local"), None)
    weights = P(("node", "local"), None, None)
    return jax.shard_map(
        on_device,
        mesh=mesh,
        in_specs=(spec, spec, spec, weights, weights),
        out_specs=spec,
        check_vma=False,
    )
```

```python
import jax
import jax.numpy as jnp
from jax import lax
from jax.experimental import pallas as pl
from jax.experimental.pallas import tpu as pltpu
from jax.sharding import PartitionSpec as P

LANES = 128
F32 = jnp.float32
BF16 = jnp.bfloat16
UP_TILE = 512
DEPTH_TILE = 512
DOWN_TILE = 512
PIECE = 512


def pack_kernel(
    route_ref, tokens_ref, out_ref, first_ref, route, tokens, low, high, source, sem
):
    top_count, row_count = route.shape
    chunks = tokens.shape[1] // LANES
    pitch = 2 * chunks
    peers = out_ref.shape[0] // pitch

    fetch_route = pltpu.make_async_copy(route_ref, route, sem.at[2])
    fetch_route.start()
    fetch = pltpu.make_async_copy(tokens_ref, tokens, sem.at[0])
    fetch.start()
    low[...] = jnp.zeros_like(low)
    high[...] = jnp.zeros_like(high)
    fetch_route.wait()
    peer = lax.broadcasted_iota(jnp.int32, (top_count, peers), 1)
    lowest = jnp.full((top_count, peers), row_count, jnp.int32)
    highest = jnp.full((top_count, peers), -1, jnp.int32)
    for t in range(row_count):
        named = route[:, t : t + 1] == peer
        lowest = jnp.where(named, jnp.minimum(lowest, t), lowest)
        highest = jnp.where(named, t, highest)
    lowest = jnp.min(lowest, axis=0, keepdims=True)
    highest = jnp.max(highest, axis=0, keepdims=True)
    second = jnp.where(highest > lowest, highest, row_count)
    side = lax.broadcasted_iota(jnp.int32, (8, peers), 0)
    first_ref[...] = jnp.where(side == 0, lowest, second)
    publish = pltpu.make_async_copy(first_ref, source, sem.at[1])
    publish.start()
    fetch.wait()
    for c in range(chunks):
        part = tokens[:, c * LANES : (c + 1) * LANES].astype(F32)
        low[pl.ds(2 * c, row_count, stride=pitch), :] = part
        high[pl.ds(2 * c + 1, row_count, stride=pitch), :] = part
    publish.wait()

    def fill(i, _):
        pair = []
        for p in (2 * i, 2 * i + 1):
            a = pl.multiple_of(source[0, p] * pitch, 8)
            b = pl.multiple_of(source[1, p] * pitch, 8)
            pair.append(low[pl.ds(a, pitch), :] + high[pl.ds(b, pitch), :])
        out_ref[pl.ds(pl.multiple_of(i * 2 * pitch, 16), 2 * pitch), :] = jnp.concatenate(
            pair, axis=0
        ).astype(BF16)
        return 0

    lax.fori_loop(0, peers // 2, fill, 0, unroll=4)


def pack(route, tokens, peers):
    row_count, width = tokens.shape
    pitch = 2 * width // LANES
    vmem = pl.BlockSpec(memory_space=pltpu.VMEM)
    anywhere = pl.BlockSpec(memory_space=pl.ANY)
    return pl.pallas_call(
        pack_kernel,
        out_shape=(
            jax.ShapeDtypeStruct((peers * pitch, LANES), BF16),
            jax.ShapeDtypeStruct((8, peers), jnp.int32),
        ),
        in_specs=[anywhere, anywhere],
        out_specs=(vmem, vmem),
        scratch_shapes=[
            pltpu.VMEM(route.shape, jnp.int32),
            pltpu.VMEM(tokens.shape, BF16),
            pltpu.VMEM(((row_count + 1) * pitch, LANES), F32),
            pltpu.VMEM(((row_count + 1) * pitch, LANES), F32),
            pltpu.SMEM((8, peers), jnp.int32),
            pltpu.SemaphoreType.DMA((3,)),
        ],
        compiler_params=pltpu.CompilerParams(vmem_limit_bytes=16 * 2**20),
        cost_estimate=pl.CostEstimate(flops=20_000_000_000, bytes_accessed=1000, transcendentals=0),
        name="pack",
    )(route, tokens)


def ffn_kernel(got_ref, gate_up_ref, down_ref, out_ref, wide, rows, active):
    width = rows.shape[1]
    hidden = active.shape[1]
    chunks = width // LANES
    pitch = 2 * chunks
    peers = got_ref.shape[0] // pitch

    def widen(i, _):
        span = pl.ds(pl.multiple_of(i * PIECE, PIECE), PIECE)
        wide[span, :] = got_ref[span, :].astype(F32)
        return 0

    lax.fori_loop(0, peers * pitch // PIECE, widen, 0)
    def build(depth):
        for c in range(depth // LANES, (depth + DEPTH_TILE) // LANES):
            for r in range(2):
                rows[r * peers : (r + 1) * peers, c * LANES : (c + 1) * LANES] = wide[
                    pl.ds(2 * c + r, peers, stride=pitch), :
                ].astype(BF16)

    for n in range(0, hidden, UP_TILE):
        if n == 0:
            gate = up = 0
            for depth in range(0, width, DEPTH_TILE):
                build(depth)
                span = slice(depth, depth + DEPTH_TILE)
                gate += jnp.dot(rows[:, span], gate_up_ref[0, span, :UP_TILE], preferred_element_type=F32)
                up += jnp.dot(
                    rows[:, span], gate_up_ref[0, span, hidden : hidden + UP_TILE], preferred_element_type=F32
                )
        else:
            gate = jnp.dot(rows[...], gate_up_ref[0, :, n : n + UP_TILE], preferred_element_type=F32)
            up = jnp.dot(rows[...], gate_up_ref[0, :, hidden + n : hidden + n + UP_TILE], preferred_element_type=F32)
        active[:, n : n + UP_TILE] = (gate / (1 + jnp.exp(-gate)) * up).astype(BF16)

    for n in range(0, width, DOWN_TILE):
        result = jnp.dot(active[...], down_ref[0, :, n : n + DOWN_TILE], preferred_element_type=F32)
        for q in range(0, DOWN_TILE, LANES):
            for r in range(2):
                wide[pl.ds(2 * (n + q) // LANES + r, peers, stride=pitch), :] = result[
                    r * peers : (r + 1) * peers, q : q + LANES
                ]

    def narrow(i, _):
        span = pl.ds(pl.multiple_of(i * PIECE, PIECE), PIECE)
        out_ref[span, :] = wide[span, :].astype(BF16)
        return 0

    lax.fori_loop(0, peers * pitch // PIECE, narrow, 0)


def expert_ffn(got, gate_up, down):
    _, width, both = gate_up.shape
    hidden = both // 2
    total = got.shape[0]
    slots = total * LANES // width
    peers = slots // 2
    return pl.pallas_call(
        ffn_kernel,
        out_shape=jax.ShapeDtypeStruct(got.shape, BF16),
        in_specs=[pl.BlockSpec(memory_space=pltpu.VMEM)] * 3,
        out_specs=pl.BlockSpec(memory_space=pltpu.VMEM),
        scratch_shapes=[
            pltpu.VMEM((total + total // peers, LANES), F32),
            pltpu.VMEM((slots, width), BF16),
            pltpu.VMEM((slots, hidden), BF16),
        ],
        compiler_params=pltpu.CompilerParams(vmem_limit_bytes=12 * 2**20),
        cost_estimate=pl.CostEstimate(
            flops=2 * slots * width * hidden * 3, bytes_accessed=6 * width * hidden, transcendentals=slots * hidden
        ),
        name="expert_ffn",
    )(got, gate_up, down)


def combine_kernel(
    route_ref, first_ref, weight_ref, got_ref, out_ref, wide, total, scale, route, first, weight, sem
):
    top_count, row_count = route.shape
    chunks = out_ref.shape[1] // LANES
    pitch = 2 * chunks
    peers = got_ref.shape[0] // pitch

    fetch_route = pltpu.make_async_copy(route_ref, route, sem.at[0])
    fetch_first = pltpu.make_async_copy(first_ref, first, sem.at[1])
    fetch_route.start()
    fetch_first.start()
    scale[...] = weight_ref[...].astype(F32)
    publish = pltpu.make_async_copy(scale, weight, sem.at[2])
    publish.start()

    def widen(i, _):
        span = pl.ds(pl.multiple_of(i * PIECE, PIECE), PIECE)
        wide[span, :] = got_ref[span, :].astype(F32)
        return 0

    lax.fori_loop(0, peers * pitch // PIECE, widen, 0)
    fetch_route.wait()
    fetch_first.wait()
    publish.wait()
    parity = lax.broadcasted_iota(jnp.int32, (8, LANES), 0) % 2

    def add_up(t, _):
        acc = jnp.zeros((pitch // 8, 8, LANES), F32)
        for k in range(top_count):
            e = route[k, t]
            start = pl.multiple_of(e * pitch, 8)
            rank = jnp.where(first[0, e] == t, 0, 1)
            factor = jnp.where(parity == rank, weight[k, t], 0.0)
            acc += wide[pl.ds(start, pitch), :].reshape(pitch // 8, 8, LANES) * factor[None]
        total[pl.ds(pl.multiple_of(t * pitch, 8), pitch), :] = acc.reshape(pitch, LANES)
        return 0

    lax.fori_loop(0, row_count, add_up, 0, unroll=4)
    for c in range(chunks):
        out_ref[:, c * LANES : (c + 1) * LANES] = (
            total[pl.ds(2 * c, row_count, stride=pitch), :] + total[pl.ds(2 * c + 1, row_count, stride=pitch), :]
        ).astype(BF16)


def combine(route, first, weight, got, width):
    row_count = route.shape[1]
    pitch = 2 * width // LANES
    anywhere = pl.BlockSpec(memory_space=pl.ANY)
    vmem = pl.BlockSpec(memory_space=pltpu.VMEM)
    return pl.pallas_call(
        combine_kernel,
        out_shape=jax.ShapeDtypeStruct((row_count, width), BF16),
        in_specs=[anywhere, anywhere, vmem, vmem],
        out_specs=vmem,
        scratch_shapes=[
            pltpu.VMEM(got.shape, F32),
            pltpu.VMEM(((row_count + 1) * pitch, LANES), F32),
            pltpu.VMEM(weight.shape, F32),
            pltpu.SMEM(route.shape, jnp.int32),
            pltpu.SMEM(first.shape, jnp.int32),
            pltpu.SMEM(weight.shape, F32),
            pltpu.SemaphoreType.DMA((3,)),
        ],
        compiler_params=pltpu.CompilerParams(vmem_limit_bytes=24 * 2**20),
        name="combine",
    )(route, first, weight, got)


def stay_in_hbm(array):
    return pltpu.with_memory_space_constraint(array, pltpu.HBM)


def exchange(blocks, peers):
    shape = blocks.shape
    blocks = blocks.reshape(peers, -1, LANES)
    return lax.all_to_all(blocks, ("node", "local"), split_axis=0, concat_axis=0, tiled=True).reshape(shape)


def on_device(tokens, route, combine_weight, gate_up, down):
    width = tokens.shape[1]
    peers = lax.axis_size("node") * lax.axis_size("local")
    route = route.T
    send, first = pack(stay_in_hbm(route), stay_in_hbm(tokens), peers)
    got = exchange(send, peers)
    result = expert_ffn(got, gate_up, down)
    back = exchange(result, peers)
    return combine(route, first, combine_weight.T, back, width)


def solution(mesh):
    spec = P(("node", "local"), None)
    weights = P(("node", "local"), None, None)
    return jax.shard_map(
        on_device,
        mesh=mesh,
        in_specs=(spec, spec, spec, weights, weights),
        out_specs=spec,
        check_vma=False,
    )
```
